32 devices in a mesh: dp: 8 (over z, x), fsdp: 4 (over y, core).
Axes of the slice: x: 2, y: 2, z: 4, core: 2. Of those that a mesh axis runs over, the one named last changes fastest.
Arguments:
- points: bfloat16 [65536, 512], P(('dp', 'fsdp')), may hold values from -8 to 8
- cotangent: bfloat16 [65536, 512], P(('dp', 'fsdp')), may hold values from -6 to 6
- destination: int32 [65536], P(('dp', 'fsdp')), may hold values from 0 to 31, as said below
- curve_slot: int32 [65536], P(('dp', 'fsdp')), may hold values from 0 to 1023, as said below
- point_counts: int32 [32], P(('dp', 'fsdp')), may hold values from 0 to 2048, as said below
- shift_offset: int32 [1], replicated, may hold values from 1 to 1023
- project_in: bfloat16 [512, 1536], P('fsdp'), may hold values from -8 to 8
- project_out: bfloat16 [512, 512], P('fsdp'), may hold values from -0.5 to 0.5
- norm_gain: bfloat16 [512], P('fsdp'), may hold values from 0.099609375 to 1.8984375
Outputs:
- block_out: bfloat16 [65536, 512], P(('dp', 'fsdp'))
- point_grad: bfloat16 [65536, 512], P(('dp', 'fsdp'))
- grad_in: float32 [512, 1536], P('fsdp')
- grad_out: float32 [512, 512], P('fsdp')
- grad_gain: float32 [512], P('fsdp')
The draws below stay inside these ranges and needn't reach their ends.
Inputs may be any that keep to these rules, and one draw needn't show every extreme that they name: Rows at or past their device's count carry no meaning. Among the counting rows of one device at most 64 name one destination, and some device sends exactly 64 to every destination. Over the counting rows of all devices every pair of destination and curve_slot occurs exactly once. `point_counts`: they sum to 32768; some device holds exactly 2048.
All inputs are finite; a program needn't handle non-finite values.
Results may differ from the reference program's by a relative error of at most 0.006.
The reference program's roundings to bfloat16 on the way count: a program that leaves them out, or rounds other values in their place, can miss the bound.
Values may be sent and summed in bfloat16 or wider, within the bound.
A program may use at most 128 MiB of HBM per device.

```python
import math
import jax
import jax.numpy as jnp
from jax import lax

D = 512
HEADS = 16
PATCH = 1024
ROWS = 1024
CAP = 64
ACQ = 2048
TOTAL = 32768
INPUT_ROWS = 65536


def routing_tables(key):
    devices = ACQ // CAP
    half = CAP // 2
    pairs = devices // 2
    keys = jax.random.split(key, 5)
    swing = jax.random.randint(keys[0], (pairs,), -(half // 2), half // 2 + 1)
    chosen = jax.random.randint(keys[1], (), 0, pairs)
    swing = jnp.where(jnp.arange(pairs) == chosen, half, swing)
    loads = jnp.stack([half + swing, half - swing], axis=1).reshape(devices)
    room = half - jnp.abs(swing) + 1
    tilt = jnp.repeat(jax.random.randint(keys[2], (pairs,), 0, 1 << 20) % room, 2)
    source = jnp.arange(devices)
    parity = 1 - 2 * ((source[:, None] + source[None, :]) % 2)
    table = loads[:, None] + tilt[:, None] * parity
    counts = jnp.sum(table, axis=1).astype(jnp.int32)
    starts = jnp.cumsum(table, axis=0) - table
    candidate = jnp.arange(ACQ)
    cand_dest = candidate // CAP
    cand_rank = candidate % CAP

    def arrange(row_key, row_table, row_starts):
        used = (cand_rank < row_table[cand_dest]).astype(jnp.int32)
        scores = (1 - used) * ACQ + jax.random.permutation(row_key, ACQ)
        picked = jnp.argsort(scores, stable=True)
        return (picked // CAP, picked % CAP, row_starts[picked // CAP])
    dest, rank, base = jax.vmap(arrange)(jax.random.split(keys[3], devices), table, starts)

    def shuffle(row_key):
        return jax.random.permutation(row_key, ROWS)
    orders = jax.vmap(shuffle)(jax.random.split(keys[4], devices))
    slot = orders[dest, (base + rank) % ROWS]
    return (dest.reshape(-1).astype(jnp.int32), slot.reshape(-1).astype(jnp.int32), counts)


def draw_destination(key, part):
    return routing_tables(key)[0]


def draw_curve_slot(key, part):
    return routing_tables(key)[1]


def draw_point_counts(key, part):
    return routing_tables(key)[2]


def draw_points(key, part):
    key = jax.random.fold_in(key, 5)
    keys = jax.random.split(key, 1)
    values = jnp.clip(jax.random.normal(keys[0], (INPUT_ROWS, D), jnp.float32), -6.0, 6.0)
    return values.astype(jnp.bfloat16)


def draw_project_in(key, part):
    key = jax.random.fold_in(key, 7)
    spread = math.sqrt(2.0 / D)
    values = jnp.clip(jax.random.normal(key, (D, 3 * D), jnp.float32), -6.0, 6.0) * spread
    return values.astype(jnp.bfloat16)


def level_of(stream_key, shape, cuts, least, high):
    def one(dim, parts):
        heights = jax.random.uniform(jax.random.fold_in(jax.random.fold_in(stream_key, 6), dim), (parts,), jnp.float32, least / len(cuts), high / len(cuts))
        return jnp.repeat(jnp.exp(heights), shape[dim] // parts).reshape((-1,) + (1,) * (len(shape) - dim - 1))

    level = one(*cuts[0])
    for cut in cuts[1:]:
        level = level * one(*cut)
    return level


def bell_draw(rng, dims, deviation, most, pieces=(), kind=jnp.bfloat16):
    factor_of = level_of(rng, dims, pieces, -0.22, 0.18) if pieces else 1.0
    drawn = jax.random.normal(rng, dims, jnp.float32) * deviation * factor_of
    return jnp.minimum(jnp.maximum(drawn, -most), most).astype(kind)


def setup_inputs(seed: int = 0) -> dict:
    key_of = jax.random.split(jax.random.key(seed), 10)
    return {
        "points": draw_points(jax.random.fold_in(key_of[9], 71), 0),
        "cotangent": bell_draw(key_of[1], (INPUT_ROWS, D), 1.0, 6.0, ((0, 32),)),
        "destination": draw_destination(jax.random.fold_in(key_of[9], 71), 0),
        "curve_slot": draw_curve_slot(jax.random.fold_in(key_of[9], 71), 0),
        "point_counts": draw_point_counts(jax.random.fold_in(key_of[9], 71), 0),
        "shift_offset": jax.random.randint(key_of[5], (1,), 1, PATCH).astype(jnp.int32),
        "project_in": draw_project_in(jax.random.fold_in(key_of[9], 71), 0),
        "project_out": bell_draw(key_of[7], (D, D), (D // 4) ** -0.5, 0.5, ((0, 4),)),
        "norm_gain": jnp.clip(1.0 + 0.18 * jax.random.normal(key_of[8], (D,), jnp.float32), 0.099609375, 1.8984375).astype(jnp.bfloat16),
    }


EPS = 1e-05

def layer_stats(values_in):
    values = values_in.astype(jnp.float32)
    center = values - lax.optimization_barrier(jnp.mean(values, axis=-1, keepdims=True))
    inverse = lax.rsqrt(lax.optimization_barrier(jnp.mean(center * center, axis=-1, keepdims=True)) + EPS)
    return (center * inverse, inverse)

def split_heads(block, heads):
    length = block.shape[0]
    head_width = block.shape[1] // heads
    group = math.gcd(heads, 4)
    shaped = block.reshape(length, heads // group, group, head_width)
    return jnp.transpose(shaped, (1, 0, 2, 3))

def join_heads(items):
    length = items.shape[1]
    return jnp.transpose(items, (1, 0, 2, 3)).reshape(length, -1)

def probabilities(query, keys, keep):
    scale = query.shape[-1] ** (-0.5)
    scores = jnp.einsum('qhe,khe->hqk', query.astype(jnp.float32), keys.astype(jnp.float32)) * scale
    scores = jnp.where(keep[None, None, :], scores, -1e+30)
    top = lax.optimization_barrier(jnp.max(scores, axis=-1, keepdims=True))
    weights = jnp.exp(scores - top)
    return weights / lax.optimization_barrier(jnp.sum(weights, axis=-1, keepdims=True))

def patch_pass(project_in, project_out, norm_gain, rows_in, cot_rows, keep):
    width = rows_in.shape[1]
    heads = HEADS
    normed, inv_std = layer_stats(rows_in)
    gain = norm_gain.astype(jnp.float32)
    hidden = (normed * gain).astype(jnp.bfloat16)
    projected = jnp.dot(hidden, project_in, preferred_element_type=jnp.float32).astype(jnp.bfloat16)
    queries = split_heads(projected[:, :width], heads)
    keyset = split_heads(projected[:, width:2 * width], heads)
    valueset = split_heads(projected[:, 2 * width:], heads)

    def forward_item(item):
        query, keys, values = item
        probs_b = probabilities(query, keys, keep).astype(jnp.bfloat16)
        return jnp.einsum('hqk,khe->qhe', probs_b.astype(jnp.float32), values.astype(jnp.float32)).astype(jnp.bfloat16)
    att_items = lax.map(forward_item, (queries, keyset, valueset))
    attended = join_heads(att_items)
    block = (rows_in.astype(jnp.float32) + jnp.dot(attended, project_out, preferred_element_type=jnp.float32)).astype(jnp.bfloat16)
    grad_att = lax.dot_general(cot_rows, project_out, (((1,), (1,)), ((), ())), preferred_element_type=jnp.float32).astype(jnp.bfloat16)
    grad_items = split_heads(grad_att, heads)

    def backward_item(item):
        query, keys, values, output, upstream = item
        scale = query.shape[-1] ** (-0.5)
        probs = probabilities(query, keys, keep)
        probs_b = probs.astype(jnp.bfloat16)
        upstream_f = upstream.astype(jnp.float32)
        along = jnp.einsum('qhe,khe->hqk', upstream_f, values.astype(jnp.float32))
        offset = lax.optimization_barrier(jnp.sum(upstream_f * output.astype(jnp.float32), axis=-1))
        slopes = (probs * (along - jnp.transpose(offset)[:, :, None]) * scale).astype(jnp.bfloat16)
        slopes_f = slopes.astype(jnp.float32)
        query_grad = jnp.einsum('hqk,khe->qhe', slopes_f, keys.astype(jnp.float32))
        key_grad = jnp.einsum('hqk,qhe->khe', slopes_f, query.astype(jnp.float32))
        value_grad = jnp.einsum('hqk,qhe->khe', probs_b.astype(jnp.float32), upstream_f)
        return (query_grad, key_grad, value_grad)
    query_grad, key_grad, value_grad = lax.map(backward_item, (queries, keyset, valueset, att_items, grad_items))
    grad_rows = jnp.concatenate([join_heads(query_grad), join_heads(key_grad), join_heads(value_grad)], axis=1).astype(jnp.bfloat16)
    grad_hidden = lax.dot_general(grad_rows, project_in, (((1,), (1,)), ((), ())), preferred_element_type=jnp.float32)
    part_in = lax.dot_general(hidden, grad_rows, (((0,), (0,)), ((), ())), preferred_element_type=jnp.float32)
    part_out = lax.dot_general(attended, cot_rows, (((0,), (0,)), ((), ())), preferred_element_type=jnp.float32)
    part_gain = lax.optimization_barrier(jnp.sum(grad_hidden * normed, axis=0))
    scaled = grad_hidden * gain
    curve_grad = cot_rows.astype(jnp.float32) + inv_std * (scaled - lax.optimization_barrier(jnp.mean(scaled, axis=-1, keepdims=True)) - normed * lax.optimization_barrier(jnp.mean(scaled * normed, axis=-1, keepdims=True)))
    return (block, curve_grad.astype(jnp.bfloat16), part_in, part_out, part_gain)

def reference(points, cotangent, destination, curve_slot, point_counts, shift_offset, project_in, project_out, norm_gain):
    width = points.shape[1]
    position = jnp.arange(INPUT_ROWS, dtype=jnp.int32)
    counting = position % ACQ < point_counts[position // ACQ]
    place = jnp.where(counting, destination * ROWS + curve_slot, TOTAL).astype(jnp.int32)
    curve_points = jnp.zeros((TOTAL, width), jnp.bfloat16).at[place].set(points, mode='drop')
    curve_cot = jnp.zeros((TOTAL, width), jnp.bfloat16).at[place].set(cotangent, mode='drop')
    front = (PATCH - shift_offset[0]).astype(jnp.int32)
    padded_len = TOTAL + PATCH
    start = (front, jnp.zeros((), jnp.int32))
    padded_points = lax.dynamic_update_slice(jnp.zeros((padded_len, width), jnp.bfloat16), curve_points, start)
    padded_cot = lax.dynamic_update_slice(jnp.zeros((padded_len, width), jnp.bfloat16), curve_cot, start)
    index = jnp.arange(padded_len, dtype=jnp.int32)
    keep = (index >= front) & (index < front + TOTAL)
    count_blocks = padded_len // PATCH

    def step(carry, inputs):
        rows_in, cot_rows, keep_rows = inputs
        block, grad_block, part_in, part_out, part_gain = patch_pass(project_in, project_out, norm_gain, rows_in, cot_rows, keep_rows)
        return ((carry[0] + part_in, carry[1] + part_out, carry[2] + part_gain), (block, grad_block))
    initial = (jnp.zeros((width, 3 * width), jnp.float32), jnp.zeros((width, width), jnp.float32), jnp.zeros((width,), jnp.float32))
    sums, outputs = lax.scan(step, initial, (padded_points.reshape(count_blocks, PATCH, width), padded_cot.reshape(count_blocks, PATCH, width), keep.reshape(count_blocks, PATCH)))
    curve_out = lax.dynamic_slice(outputs[0].reshape(padded_len, width), start, (TOTAL, width))
    curve_grad = lax.dynamic_slice(outputs[1].reshape(padded_len, width), start, (TOTAL, width))
    safe = jnp.minimum(place, TOTAL - 1)
    block_out = jnp.where(counting[:, None], curve_out[safe], jnp.zeros((), jnp.bfloat16))
    point_grad = jnp.where(counting[:, None], curve_grad[safe], jnp.zeros((), jnp.bfloat16))
    return (block_out, point_grad, sums[0], sums[1], sums[2])
```

```python
import functools
import math

import jax
import jax.numpy as jnp
from jax import lax
from jax.experimental import pallas as pl
from jax.experimental.pallas import tpu as pltpu
from jax.sharding import PartitionSpec as P

HEADS = 16
PATCH = 1024
EPS = 1e-05
AXES = ("dp", "fsdp")
FAR = -1e30


def layer_stats(values_in):
    values = values_in.astype(jnp.float32)
    center = values - jnp.mean(values, axis=-1, keepdims=True)
    inverse = lax.rsqrt(jnp.mean(center * center, axis=-1, keepdims=True) + EPS)
    return (center * inverse, inverse)


def attention_kernel(
    head_width,
    q_ref,
    k_ref,
    v_ref,
    g_ref,
    qt_ref,
    kt_ref,
    vt_ref,
    gt_ref,
    kcode_ref,
    qcode_ref,
    ot_ref,
    dqt_ref,
    dk_ref,
    dv_ref,
    dk_sum,
    dv_sum,
):
    rows, lanes = q_ref.shape
    block = 256
    heads = lanes // head_width
    scale = head_width ** (-0.5)
    rate = scale * math.log2(math.e)
    dk_sum[...] = jnp.zeros_like(dk_sum)
    dv_sum[...] = jnp.zeros_like(dv_sum)

    def step(index, carry):
        cols = pl.ds(pl.multiple_of(index * block, block), block)
        queries_t = qt_ref[:, cols]
        upstream_t = gt_ref[:, cols]
        queries = q_ref[cols, :]
        upstream = g_ref[cols, :]
        qcode = qcode_ref[:, cols]
        across = lax.broadcasted_iota(jnp.int32, (lanes, block), 0) // head_width
        along = lax.broadcasted_iota(jnp.int32, (block, lanes), 1) // head_width
        none = jnp.zeros((), jnp.bfloat16)
        for head in range(heads):
            part = slice(head * head_width, (head + 1) * head_width)
            keys = jnp.concatenate([k_ref[...], kcode_ref[...]], axis=1)
            one_t = jnp.concatenate([jnp.where(across == head, queries_t, none), qcode], axis=0)
            scores = jnp.dot(keys, one_t, preferred_element_type=jnp.float32)
            top = jnp.max(scores, axis=0, keepdims=True)
            weights = jnp.exp2((scores - top) * rate)
            total = jnp.sum(weights, axis=0, keepdims=True)
            probs = weights * (1.0 / total)
            probs_b = probs.astype(jnp.bfloat16)
            out_t = jnp.dot(
                vt_ref[part, :], probs_b, preferred_element_type=jnp.float32
            ).astype(jnp.bfloat16)
            ot_ref[part, cols] = out_t
            offset = jnp.sum(
                upstream_t[part, :].astype(jnp.float32) * out_t.astype(jnp.float32),
                axis=0,
                keepdims=True,
            )
            forward = jnp.dot(
                v_ref[...],
                jnp.where(across == head, upstream_t, none),
                preferred_element_type=jnp.float32,
            )
            slopes = (probs * ((forward - offset) * scale)).astype(jnp.bfloat16)
            dqt_ref[part, cols] = jnp.dot(
                kt_ref[part, :], slopes, preferred_element_type=jnp.float32
            ).astype(jnp.bfloat16)
            dk_sum[...] += jnp.dot(
                slopes,
                jnp.where(along == head, queries, none),
                preferred_element_type=jnp.float32,
            )
            dv_sum[...] += jnp.dot(
                probs_b,
                jnp.where(along == head, upstream, none),
                preferred_element_type=jnp.float32,
            )
        return carry

    lax.fori_loop(0, rows // block, step, 0)
    dk_ref[...] = dk_sum[...].astype(jnp.bfloat16)
    dv_ref[...] = dv_sum[...].astype(jnp.bfloat16)


def attention(projected, projected_t, grad_att, grad_att_t, kcode, qcode):
    rows, width = grad_att.shape
    lanes = 128
    groups = width // lanes
    head_width = width // HEADS

    def tall(offset):
        return pl.BlockSpec((rows, lanes), lambda i: (0, offset * groups + i))

    def wide(offset):
        return pl.BlockSpec((lanes, rows), lambda i: (offset * groups + i, 0))

    flops = 12 * rows * rows * width
    return pl.pallas_call(
        functools.partial(attention_kernel, head_width),
        grid=(groups,),
        in_specs=[
            tall(0),
            tall(1),
            tall(2),
            tall(0),
            wide(0),
            wide(1),
            wide(2),
            wide(0),
            pl.BlockSpec((rows, lanes), lambda i: (0, 0)),
            pl.BlockSpec((lanes, rows), lambda i: (0, 0)),
        ],
        out_specs=[wide(0), wide(0), tall(0), tall(0)],
        out_shape=[
            jax.ShapeDtypeStruct((width, rows), jnp.bfloat16),
            jax.ShapeDtypeStruct((width, rows), jnp.bfloat16),
            jax.ShapeDtypeStruct((rows, width), jnp.bfloat16),
            jax.ShapeDtypeStruct((rows, width), jnp.bfloat16),
        ],
        scratch_shapes=[
            pltpu.VMEM((rows, lanes), jnp.float32),
            pltpu.VMEM((rows, lanes), jnp.float32),
        ],
        compiler_params=pltpu.CompilerParams(vmem_limit_bytes=48 * 2**20),
        cost_estimate=pl.CostEstimate(
            flops=flops, bytes_accessed=20 * rows * width, transcendentals=rows * rows * HEADS
        ),
    )(
        projected,
        projected,
        projected,
        grad_att,
        projected_t,
        projected_t,
        projected_t,
        grad_att_t,
        kcode,
        qcode,
    )


def dot(left, right, dims, kind=jnp.float32):
    return lax.dot_general(
        left, right, (dims, ((), ())), preferred_element_type=jnp.float32
    ).astype(kind)


def patch_work(rows_in, cot_in, in_first, own_codes, full_in, full_out, full_gain):
    rows, width = rows_in.shape
    normed, inv_std = layer_stats(rows_in)
    gain = full_gain.astype(jnp.float32)
    hidden = (normed * gain).astype(jnp.bfloat16)
    projected = dot(hidden, full_in, ((1,), (0,)), jnp.bfloat16)
    projected_t = dot(full_in, hidden, ((0,), (1,)), jnp.bfloat16)
    grad_att = dot(cot_in, full_out, ((1,), (1,)), jnp.bfloat16)
    grad_att_t = dot(full_out, cot_in, ((1,), (1,)), jnp.bfloat16)
    lane = jnp.arange(128, dtype=jnp.int32)
    first = in_first | jnp.logical_not(own_codes)
    kind = jnp.where(first, 0, 1)
    kcode = (lane[None, :] == kind[:, None]).astype(jnp.bfloat16)
    qcode = jnp.where(lane[:, None] == 1 - kind[None, :], FAR, 0.0).astype(jnp.bfloat16)
    att_t, dq_t, dk, dv = attention(projected, projected_t, grad_att, grad_att_t, kcode, qcode)
    curve_out = (
        rows_in.astype(jnp.float32) + dot(att_t, full_out, ((0,), (0,)))
    ).astype(jnp.bfloat16)
    grad_rows = jnp.concatenate([dq_t.T, dk, dv], axis=1)
    grad_hidden = dot(grad_rows, full_in, ((1,), (1,)))
    part_in = dot(hidden, grad_rows, ((0,), (0,)))
    part_out = dot(att_t, cot_in, ((1,), (0,)))
    part_gain = jnp.sum(grad_hidden * normed, axis=0)
    scaled = grad_hidden * gain
    curve_grad = (
        cot_in.astype(jnp.float32)
        + inv_std
        * (
            scaled
            - jnp.mean(scaled, axis=-1, keepdims=True)
            - normed * jnp.mean(scaled * normed, axis=-1, keepdims=True)
        )
    ).astype(jnp.bfloat16)
    return (curve_out, curve_grad, part_in, part_out, part_gain)


def regroup(rows, devices):
    shaped = rows.reshape(devices, rows.shape[0] // devices, rows.shape[1])
    return lax.all_to_all(shaped, AXES, split_axis=0, concat_axis=0, tiled=True).reshape(rows.shape)


def body(
    points,
    cotangent,
    destination,
    curve_slot,
    point_counts,
    shift_offset,
    project_in,
    project_out,
    norm_gain,
):
    devices = lax.axis_size(AXES)
    me = lax.axis_index(AXES)
    arrived, width = points.shape
    capacity = arrived // devices
    slots = devices * capacity
    own_rows = arrived // 2
    half = own_rows // 2
    shift = shift_offset[0]
    full_in = lax.all_gather(project_in, "fsdp", axis=0, tiled=True)
    full_out = lax.all_gather(project_out, "fsdp", axis=0, tiled=True)
    full_gain = lax.all_gather(norm_gain, "fsdp", axis=0, tiled=True)

    order = jnp.arange(arrived, dtype=jnp.int32)
    valid = order < point_counts[0]
    earlier = (
        (destination[None, :] == destination[:, None])
        & valid[None, :]
        & (order[None, :] < order[:, None])
    )
    ranking = jnp.sum(earlier.astype(jnp.int32), axis=1)
    target = jnp.where(valid, destination * capacity + ranking, slots)
    slot_order = jnp.arange(slots, dtype=jnp.int32)
    pick = (slot_order[:, None] == target[None, :]).astype(jnp.bfloat16)
    rolled_slot = (curve_slot - shift) & (own_rows - 1)
    digits = jnp.stack([rolled_slot // 64 + 1, rolled_slot % 64], axis=1).astype(jnp.bfloat16)
    marks = dot(pick, digits, ((1,), (0,)), jnp.bfloat16)
    both = jnp.concatenate([points, cotangent], axis=1)
    sent = dot(pick, both, ((1,), (0,)), jnp.bfloat16)
    got_marks = regroup(marks, devices).astype(jnp.int32)
    got = regroup(sent, devices)
    landing = jnp.where(
        got_marks[:, 0] > 0, (got_marks[:, 0] - 1) * 64 + got_marks[:, 1], own_rows
    )
    place = jnp.arange(own_rows, dtype=jnp.int32)
    spread = (place[:, None] == landing[None, :]).astype(jnp.bfloat16)
    rolled = dot(spread, got, ((1,), (0,)), jnp.bfloat16)

    ahead = [(i, (i + 1) % devices) for i in range(devices)]
    behind = [((i + 1) % devices, i) for i in range(devices)]
    late = shift >= half
    in_first = place < own_rows - shift
    low, high = rolled[:half], rolled[half:]
    from_behind = lax.ppermute(low, AXES, ahead)
    from_ahead = lax.ppermute(high, AXES, behind)
    low_in = jnp.where((late & in_first[:half])[:, None], from_behind, low)
    high_in = jnp.where((~late & ~in_first[half:])[:, None], from_ahead, high)
    curve = jnp.concatenate([low_in, high_in], axis=0)
    seam = jnp.where(late, me == 0, me == devices - 1)

    curve_out, curve_grad, part_in, part_out, part_gain = patch_work(
        curve[:, :width], curve[:, width:], in_first, seam, full_in, full_out, full_gain
    )
    results = jnp.concatenate([curve_out, curve_grad], axis=1)
    low, high = results[:half], results[half:]
    from_ahead = lax.ppermute(low, AXES, behind)
    from_behind = lax.ppermute(high, AXES, ahead)
    low = jnp.where((late & in_first[:half])[:, None], from_ahead, low)
    high = jnp.where((~late & ~in_first[half:])[:, None], from_behind, high)
    results = jnp.concatenate([low, high], axis=0)

    part_gain = jnp.broadcast_to(part_gain[:, None], (width, 128))
    parts = jnp.concatenate([part_in, part_out, part_gain], axis=1)
    shares = lax.psum_scatter(parts, "fsdp", scatter_dimension=0, tiled=True)
    totals = lax.psum(shares, "dp")
    picked = dot(spread, results, ((0,), (0,)), jnp.bfloat16)
    back = regroup(picked, devices)
    returned = dot(pick, back, ((0,), (0,)), jnp.bfloat16)
    return (
        returned[:, :width],
        returned[:, width:],
        totals[:, : 3 * width],
        totals[:, 3 * width : 4 * width],
        totals[:, 4 * width],
    )


def solution(mesh):
    in_specs = (
        P(AXES, None),
        P(AXES, None),
        P(AXES),
        P(AXES),
        P(AXES),
        P(),
        P("fsdp", None),
        P("fsdp", None),
        P("fsdp"),
    )
    out_specs = (P(AXES, None), P(AXES, None), P("fsdp", None), P("fsdp", None), P("fsdp"))
    return jax.shard_map(body, mesh=mesh, in_specs=in_specs, out_specs=out_specs, check_vma=False)
```
